32 devices in a mesh: cx: 4 (over y, x), cy: 8 (over z, core).
Axes of the slice: x: 2, y: 2, z: 4, core: 2. Of those that a mesh axis runs over, the one named last changes fastest.
Arguments:
- query_rows: bfloat16 [8192, 1024], P(('cx', 'cy')), may hold values from -6 to 6
- key_rows: bfloat16 [8192, 1024], P(('cx', 'cy')), may hold values from -6 to 6
- value_rows: bfloat16 [8192, 1024], P(('cx', 'cy')), may hold values from -6 to 6
- forward_out: bfloat16 [8192, 1024], P(('cx', 'cy')), may hold values from -6 to 6
- out_grad: bfloat16 [8192, 1024], P(('cx', 'cy')), may hold values from -6 to 6
- doc_blocks: int32 [8], replicated, may hold values from 1 to 15, 64 in all
Outputs:
- query_grad: bfloat16 [8192, 1024], P(('cx', 'cy'))
- key_grad: bfloat16 [8192, 1024], P(('cx', 'cy'))
- value_grad: bfloat16 [8192, 1024], P(('cx', 'cy'))
The draws below stay inside these ranges and needn't reach their ends.
Inputs may be any that keep to these rules, and one draw needn't show every extreme that they name: `doc_blocks`: lengths of the documents in blocks of 128 tokens, in sequence order, summing to 64; the longest has exactly 15 blocks.
All inputs are finite; a program needn't handle non-finite values.
Results may differ from the reference program's by a relative error of at most 0.0049.
Values may be sent and summed in bfloat16 or wider, within the bound.
A program may use at most 128 MiB of HBM per device.

```python
import math
import jax
import jax.numpy as jnp
import numpy as np
from jax import lax

HEADS = 8
DH = 128
TOK_DEV = 256
BLOCK = 128
REACH = 7
TOKENS = 8192
MOST_BLOCKS = 15
NDOC = 8


def drawn_pair(key):
    shape = (TOKENS, HEADS * DH)
    queries = jax.random.normal(jax.random.fold_in(key, 11), shape, jnp.float32)
    keys_out = jax.random.normal(jax.random.fold_in(key, 12), shape, jnp.float32)
    return (jnp.clip(queries, -6.0, 6.0), jnp.clip(keys_out, -6.0, 6.0))


def draw_query_rows(key, part):
    return drawn_pair(key)[0].astype(jnp.bfloat16)


def draw_key_rows(key, part):
    return drawn_pair(key)[1].astype(jnp.bfloat16)


def level_of(rng, shape, split, smallest, top_value):
    factor_of = 1.0
    for dim, parts in split:
        draws = jax.random.uniform(jax.random.fold_in(jax.random.fold_in(rng, 6), dim), (parts,), jnp.float32, smallest / len(split), top_value / len(split))
        factor_of = factor_of * jnp.repeat(jnp.exp(draws), shape[dim] // parts).reshape((-1,) + (1,) * (len(shape) - 1 - dim))
    return factor_of


def profile(count, total, reach, lean):
    loads = [(1 << 20) // math.isqrt(rank ** lean) + 1 for rank in range(2, count + 1)]
    rest, holding = total - reach - (count - 1), [1] * (count - 1)
    while rest > 0:
        free = [i for i in range(count - 1) if holding[i] < reach]
        pool, budget = sum([loads[i] for i in free]), rest
        for i in free:
            extra = min(reach - holding[i], max(1, budget * loads[i] // pool), rest)
            holding[i] = holding[i] + extra
            rest = rest - extra
    return np.array([reach] + holding)


def ragged_sizes(key, amount, total, limit, skew):
    if amount == 2:
        one = jax.random.randint(key, (), max(1, total - limit), min(limit, total - 1) + 1)
        return jnp.stack([one, total - one])
    tallies = jnp.asarray(profile(amount, total, limit, skew), jnp.int32)
    couples = (amount - 1) // 2
    donor, sink = tallies[1:1 + 2 * couples:2], tallies[2:2 + 2 * couples:2]
    room = jnp.minimum(donor - 1, limit - sink)
    passed = jax.random.randint(jax.random.fold_in(key, 1), (couples,), 0, 1 << 20) % (room + 1)
    tallies = tallies.at[1:1 + 2 * couples:2].set(donor - passed).at[2:2 + 2 * couples:2].set(sink + passed)
    return tallies[jax.random.permutation(jax.random.fold_in(key, 2), amount)]


def centred(own_key, shape, scale, limit, split=(), kind=jnp.bfloat16):
    drawn = scale * jax.random.normal(own_key, shape, jnp.float32)
    if split:
        drawn = drawn * level_of(own_key, shape, split, -0.22, 0.18)
    return jnp.clip(drawn, -limit, limit).astype(kind)


def setup_inputs(seed: int = 0) -> dict:
    key_list = jax.random.split(jax.random.key(seed), 7)
    query_rows = draw_query_rows(jax.random.fold_in(key_list[6], 71), 0)
    key_rows = draw_key_rows(jax.random.fold_in(key_list[6], 71), 0)
    value_rows = centred(key_list[2], (TOKENS, HEADS * DH), 1.0, 6.0, ((0, 32),))
    forward_out = centred(key_list[3], (TOKENS, HEADS * DH), 1.0, 6.0, ((0, 32),))
    out_grad = centred(key_list[4], (TOKENS, HEADS * DH), 1.0, 6.0, ((0, 32),))
    doc_blocks = ragged_sizes(key_list[5], NDOC, TOKENS // BLOCK, MOST_BLOCKS, 1).astype(jnp.int32)
    return dict(query_rows=query_rows, key_rows=key_rows, value_rows=value_rows, forward_out=forward_out, out_grad=out_grad, doc_blocks=doc_blocks)


def doc_ids(doc_blocks, nblocks):
    ends = jnp.cumsum(doc_blocks).astype(jnp.int32)
    starts = ends - doc_blocks.astype(jnp.int32)
    block_ids = jnp.arange(nblocks, dtype=jnp.int32)
    return (lax.optimization_barrier(jnp.sum((starts[None, :] <= block_ids[:, None]).astype(jnp.int32), axis=1)) - 1).astype(jnp.int32)

def reference(query_rows, key_rows, value_rows, forward_out, out_grad, doc_blocks):
    rows = TOK_DEV
    shards = TOKENS // rows
    features = HEADS * DH
    scale = 1.0 / math.sqrt(DH)
    margin = REACH * rows
    token_docs = jnp.repeat(doc_ids(doc_blocks, TOKENS // BLOCK), BLOCK).astype(jnp.int32)
    padded_docs = jnp.concatenate([jnp.full((margin,), -1, jnp.int32), token_docs])
    padded_keys = jnp.concatenate([jnp.zeros((margin, features), key_rows.dtype), key_rows])
    padded_values = jnp.concatenate([jnp.zeros((margin, features), value_rows.dtype), value_rows])

    def one_shard(carry, shard):
        key_acc, value_acc = carry
        start = (shard * rows).astype(jnp.int32)
        query = lax.dynamic_slice_in_dim(query_rows, start, rows, 0).astype(jnp.float32).reshape(rows, HEADS, DH)
        grads = lax.dynamic_slice_in_dim(out_grad, start, rows, 0).astype(jnp.float32).reshape(rows, HEADS, DH)
        outs = lax.dynamic_slice_in_dim(forward_out, start, rows, 0).astype(jnp.float32).reshape(rows, HEADS, DH)
        keys_win = lax.dynamic_slice_in_dim(padded_keys, start, margin + rows, 0).astype(jnp.float32).reshape(margin + rows, HEADS, DH)
        values_win = lax.dynamic_slice_in_dim(padded_values, start, margin + rows, 0).astype(jnp.float32).reshape(margin + rows, HEADS, DH)
        query_docs = lax.dynamic_slice_in_dim(token_docs, start, rows, 0)
        key_docs = lax.dynamic_slice_in_dim(padded_docs, start, margin + rows, 0)
        query_pos = jnp.arange(rows, dtype=jnp.int32) + margin
        key_pos = jnp.arange(margin + rows, dtype=jnp.int32)
        mask = (query_docs[:, None] == key_docs[None, :]) & (key_pos[None, :] <= query_pos[:, None])
        scores = jnp.einsum('qhd,khd->hqk', query, keys_win) * scale
        masked = jnp.where(mask[None], scores, -1e+30)
        top = lax.optimization_barrier(jnp.max(masked, axis=2))
        logsum = top + jnp.log(lax.optimization_barrier(jnp.sum(jnp.exp(masked - top[..., None]), axis=2)))
        prob = jnp.where(mask[None], jnp.exp(masked - logsum[..., None]), 0.0)
        prob_b = prob.astype(jnp.bfloat16).astype(jnp.float32)
        delta = jnp.einsum('qhd,qhd->hq', grads, outs)
        dprob = jnp.einsum('qhd,khd->hqk', grads, values_win)
        dscore = (prob * (dprob - delta[..., None])).astype(jnp.bfloat16).astype(jnp.float32)
        query_part = jnp.einsum('hqk,khd->qhd', dscore, keys_win) * scale
        key_part = (jnp.einsum('hqk,qhd->khd', dscore, query) * scale).reshape(margin + rows, features)
        value_part = jnp.einsum('hqk,qhd->khd', prob_b, grads).reshape(margin + rows, features)
        old_keys = lax.dynamic_slice_in_dim(key_acc, start, margin + rows, 0)
        old_values = lax.dynamic_slice_in_dim(value_acc, start, margin + rows, 0)
        key_acc = lax.dynamic_update_slice_in_dim(key_acc, old_keys + key_part, start, 0)
        value_acc = lax.dynamic_update_slice_in_dim(value_acc, old_values + value_part, start, 0)
        return ((key_acc, value_acc), query_part.reshape(rows, features).astype(jnp.bfloat16))
    empty = jnp.zeros((margin + TOKENS, features), jnp.float32)
    (key_acc, value_acc), query_parts = lax.scan(one_shard, (empty, empty), jnp.arange(shards, dtype=jnp.int32))
    query_grad = query_parts.reshape(TOKENS, features)
    return (query_grad, key_acc[margin:].astype(jnp.bfloat16), value_acc[margin:].astype(jnp.bfloat16))
```

```python
import math

import jax
import jax.numpy as jnp
from jax import lax
from jax.experimental import pallas as pl
from jax.experimental.pallas import tpu as pltpu
from jax.sharding import PartitionSpec as P

HEADS = 8
DH = 128
BLOCK = 128
REACH = 7
GROUP = 8
MESH = pl.DeviceIdType.MESH
NT = (((1,), (1,)), ((), ()))
TN = (((0,), (0,)), ((), ()))


def place():
    inner = lax.axis_size("cy")
    count = lax.axis_size("cx") * inner
    shard = lax.axis_index("cx") * inner + lax.axis_index("cy")

    def device(index):
        return (index // inner, lax.rem(index, inner))

    return count, shard, device


def rows_at(index, rows):
    return pl.ds(pl.multiple_of(index * rows, rows), rows)


def cols_at(head):
    return pl.ds(pl.multiple_of(head * DH, DH), DH)


def spread_kernel(
    q_ref, k_ref, v_ref, o_ref, g_ref, qh, gh, kw, vw, dh, dsend, send, recv, fsend, frecv, local
):
    rows = q_ref.shape[0]
    count, shard, device = place()
    me = lax.rem(shard, GROUP)
    base = shard - me
    ahead = device(lax.rem(shard + GROUP, count))
    behind = device(lax.rem(shard + count - GROUP, count))
    barrier = pltpu.get_barrier_semaphore()
    for j in range(1, GROUP):
        peer = device(base + lax.rem(me + j, GROUP))
        pl.semaphore_signal(barrier, inc=1, device_id=peer, device_id_type=MESH)
    pl.semaphore_signal(barrier, inc=1, device_id=behind, device_id_type=MESH)
    pl.semaphore_wait(barrier, GROUP)

    tensors = ((k_ref, kw, REACH), (v_ref, vw, REACH), (q_ref, qh, 0), (g_ref, gh, 0))

    def out_copy(which, j):
        src, dst, shift = tensors[which]
        peer = lax.rem(me + j, GROUP)
        return pltpu.make_async_remote_copy(
            src_ref=src.at[:, cols_at(peer)],
            dst_ref=dst.at[rows_at(me + shift, rows), :],
            send_sem=send.at[which, j],
            recv_sem=recv.at[which, j],
            device_id=device(base + peer),
            device_id_type=MESH,
        )

    def in_copy(which, j):
        src, dst, shift = tensors[which]
        peer = lax.rem(me + GROUP - j, GROUP)
        return pltpu.make_async_remote_copy(
            src_ref=src.at[:, cols_at(peer)],
            dst_ref=dst.at[rows_at(peer + shift, rows), :],
            send_sem=send.at[which, j],
            recv_sem=recv.at[which, j],
            device_id=device(base + peer),
            device_id_type=MESH,
        )

    def own_copy(which):
        src, dst, shift = tensors[which]
        return pltpu.make_async_copy(
            src.at[:, cols_at(me)], dst.at[rows_at(me + shift, rows), :], local.at[which]
        )

    def forward(which, shard_in_group):
        _, dst, shift = tensors[which]
        return pltpu.make_async_remote_copy(
            src_ref=dst.at[rows_at(shard_in_group + shift, rows), :],
            dst_ref=dst.at[rows_at(shard_in_group - 1, rows), :],
            send_sem=fsend.at[which, shard_in_group],
            recv_sem=frecv.at[which, shard_in_group],
            device_id=ahead,
            device_id_type=MESH,
        )

    for which in range(4):
        own_copy(which).start()
    for which in range(4):
        for j in range(1, GROUP):
            out_copy(which, j).start()

    ones = jnp.ones((8, DH), jnp.bfloat16)
    for head in range(HEADS):
        cols = slice(head * DH, (head + 1) * DH)
        product = g_ref[:, cols].astype(jnp.float32) * o_ref[:, cols].astype(jnp.float32)
        high = product.astype(jnp.bfloat16)
        low = (product - high.astype(jnp.float32)).astype(jnp.bfloat16)
        dsend[head] = lax.dot_general(
            ones, high, NT, preferred_element_type=jnp.float32
        ) + lax.dot_general(ones, low, NT, preferred_element_type=jnp.float32)

    def delta_copy(j, peer, source):
        return pltpu.make_async_remote_copy(
            src_ref=dsend.at[peer],
            dst_ref=dh.at[source],
            send_sem=send.at[4, j],
            recv_sem=recv.at[4, j],
            device_id=device(base + peer),
            device_id_type=MESH,
        )

    own_delta = pltpu.make_async_copy(dsend.at[me], dh.at[me], local.at[4])
    own_delta.start()
    for j in range(1, GROUP):
        delta_copy(j, lax.rem(me + j, GROUP), me).start()

    for which in range(2):
        own_copy(which).wait()

    @pl.when(me >= 1)
    def _():
        for which in range(2):
            forward(which, me).start()

    for j in range(1, GROUP):
        source = lax.rem(me + GROUP - j, GROUP)
        for which in range(2):
            in_copy(which, j).wait_recv()

        @pl.when(source >= 1)
        def _():
            for which in range(2):
                forward(which, source).start()

    for which in range(2, 4):
        own_copy(which).wait()
        for j in range(1, GROUP):
            in_copy(which, j).wait_recv()
    own_delta.wait()
    for j in range(1, GROUP):
        peer = lax.rem(me + GROUP - j, GROUP)
        delta_copy(j, peer, peer).wait_recv()
    for s in range(1, GROUP):
        for which in range(2):
            forward(which, s).wait_recv()
    for s in range(1, GROUP):
        for which in range(2):
            forward(which, s).wait_send()
    for j in range(1, GROUP):
        for which in range(4):
            out_copy(which, j).wait_send()
        delta_copy(j, lax.rem(me + j, GROUP), me).wait_send()


def grad_kernel(
    docs, q_ref, g_ref, k_ref, v_ref, d_ref, dq_ref, dk_ref, dv_ref, hk_ref, hv_ref, dk, dv, keep
):
    ndoc = docs.shape[0]
    rows = q_ref.shape[0] // GROUP
    per_tile = rows // BLOCK
    scale = 1.0 / math.sqrt(DH)
    _, shard, _ = place()
    group_block = (shard - lax.rem(shard, GROUP)) * per_tile
    dk[...] = jnp.zeros_like(dk)
    dv[...] = jnp.zeros_like(dv)
    key_at = lax.broadcasted_iota(jnp.int32, (rows, rows), 0)
    query_at = lax.broadcasted_iota(jnp.int32, (rows, rows), 1)
    lane = lax.broadcasted_iota(jnp.int32, (1, rows), 1)

    def tile(i, _):
        first_block = group_block + i * per_tile

        def look(n, state):
            start, firsts = state
            firsts = tuple(
                jnp.where(start <= first_block + b, start, firsts[b]) for b in range(per_tile)
            )
            return start + docs[n], firsts

        _, firsts = lax.fori_loop(
            0, ndoc, look, (jnp.int32(0), tuple(jnp.int32(0) for _ in range(per_tile)))
        )
        firsts = [f - group_block + REACH * per_tile for f in firsts]
        begin = firsts[0] // per_tile
        end = i + REACH + 1
        start_row = jnp.full((1, rows), 0, jnp.int32)
        for b in range(per_tile):
            start_row = jnp.where(lane >= b * BLOCK, firsts[b] * BLOCK, start_row)
        q = q_ref[rows_at(i, rows), :]
        g = g_ref[rows_at(i, rows), :]
        delta = d_ref[i, 0:1, :]
        last_row = (i + REACH) * rows + lane

        def scores(j, top):
            s = lax.dot_general(
                k_ref[rows_at(j, rows), :], q, NT, preferred_element_type=jnp.float32
            )
            at = key_at + j * rows
            s = jnp.where((at >= start_row) & (at <= last_row), s * scale, -1e30)
            keep[j - begin] = s
            return jnp.maximum(top, jnp.max(s, axis=0, keepdims=True))

        top = lax.fori_loop(begin, end, scores, jnp.full((1, rows), -1e30, jnp.float32))

        def sums(j, total):
            p = jnp.exp(keep[j - begin] - top)
            keep[j - begin] = p
            return total + jnp.sum(p, axis=0, keepdims=True)

        total = lax.fori_loop(begin, end, sums, jnp.zeros((1, rows), jnp.float32))
        inverse = 1.0 / total

        def grads(j, dq):
            at = rows_at(j, rows)
            k = k_ref[at, :]
            prob = keep[j - begin] * inverse
            dprob = lax.dot_general(v_ref[at, :], g, NT, preferred_element_type=jnp.float32)
            ds = (prob * (dprob - delta)).astype(jnp.bfloat16)
            dv[at, :] += jnp.dot(prob.astype(jnp.bfloat16), g, preferred_element_type=jnp.float32)
            dk[at, :] += jnp.dot(ds, q, preferred_element_type=jnp.float32)
            return dq + lax.dot_general(ds, k, TN, preferred_element_type=jnp.float32)

        dq = lax.fori_loop(begin, end, grads, jnp.zeros((rows, DH), jnp.float32))
        dq_ref[rows_at(i, rows), :] = (dq * scale).astype(jnp.bfloat16)
        return 0

    lax.fori_loop(0, GROUP, tile, 0)
    halo = REACH * rows
    hk_ref[...] = (dk[:halo, :] * scale).astype(jnp.bfloat16)
    hv_ref[...] = dv[:halo, :].astype(jnp.bfloat16)
    dk_ref[...] = dk[halo:, :] * scale
    dv_ref[...] = dv[halo:, :]


def collect_kernel(
    dq_ref, dk_ref, dv_ref, hk_ref, hv_ref, qo, ko, vo, hk, hv, ks, vs, send, recv, hsend, hrecv, local
):
    rows = qo.shape[0]
    count, shard, device = place()
    me = lax.rem(shard, GROUP)
    base = shard - me
    ahead = device(lax.rem(shard + GROUP, count))
    behind = device(lax.rem(shard + count - GROUP, count))
    barrier = pltpu.get_barrier_semaphore()
    for j in range(1, GROUP):
        peer = device(base + lax.rem(me + j, GROUP))
        pl.semaphore_signal(barrier, inc=1, device_id=peer, device_id_type=MESH)
    pl.semaphore_signal(barrier, inc=1, device_id=ahead, device_id_type=MESH)
    pl.semaphore_wait(barrier, GROUP)

    halos = ((hk_ref, hk), (hv_ref, hv))

    def halo_copy(which, s):
        src, dst = halos[which]
        at = rows_at(s - 1, rows)
        return pltpu.make_async_remote_copy(
            src_ref=src.at[at, :],
            dst_ref=dst.at[at, :],
            send_sem=hsend.at[which, s],
            recv_sem=hrecv.at[which, s],
            device_id=behind,
            device_id_type=MESH,
        )

    tensors = ((dq_ref, qo), (ks, ko), (vs, vo))

    def out_copy(which, j):
        src, dst = tensors[which]
        peer = lax.rem(me + j, GROUP)
        return pltpu.make_async_remote_copy(
            src_ref=src.at[rows_at(peer, rows), :],
            dst_ref=dst.at[:, cols_at(me)],
            send_sem=send.at[which, j],
            recv_sem=recv.at[which, j],
            device_id=device(base + peer),
            device_id_type=MESH,
        )

    def in_copy(which, j):
        src, dst = tensors[which]
        peer = lax.rem(me + GROUP - j, GROUP)
        return pltpu.make_async_remote_copy(
            src_ref=src.at[rows_at(peer, rows), :],
            dst_ref=dst.at[:, cols_at(peer)],
            send_sem=send.at[which, j],
            recv_sem=recv.at[which, j],
            device_id=device(base + peer),
            device_id_type=MESH,
        )

    def own_copy(which):
        src, dst = tensors[which]
        return pltpu.make_async_copy(
            src.at[rows_at(me, rows), :], dst.at[:, cols_at(me)], local.at[which]
        )

    for j in range(GROUP):
        s = lax.rem(me + j, GROUP)

        @pl.when(s >= 1)
        def _():
            for which in range(2):
                halo_copy(which, s).start()

    own_copy(0).start()
    for j in range(1, GROUP):
        out_copy(0, j).start()

    for j in [*range(1, GROUP), 0]:
        s = lax.rem(me + j, GROUP)
        at = rows_at(s, rows)

        @pl.when(s == 0)
        def _():
            ks[at, :] = dk_ref[at, :].astype(jnp.bfloat16)
            vs[at, :] = dv_ref[at, :].astype(jnp.bfloat16)

        @pl.when(s >= 1)
        def _():
            before = rows_at(s - 1, rows)
            halo_copy(0, s).wait_recv()
            ks[at, :] = (dk_ref[at, :] + hk[before, :].astype(jnp.float32)).astype(jnp.bfloat16)
            halo_copy(1, s).wait_recv()
            vs[at, :] = (dv_ref[at, :] + hv[before, :].astype(jnp.float32)).astype(jnp.bfloat16)

        for which in (1, 2):
            if j:
                out_copy(which, j).start()
            else:
                own_copy(which).start()

    for which in range(3):
        own_copy(which).wait()
        for j in range(1, GROUP):
            in_copy(which, j).wait_recv()
    for which in range(3):
        for j in range(1, GROUP):
            out_copy(which, j).wait_send()
    for s in range(1, GROUP):
        for which in range(2):
            halo_copy(which, s).wait_send()


def per_device(query_rows, key_rows, value_rows, forward_out, out_grad, doc_blocks):
    rows, features = query_rows.shape
    bf16, f32 = jnp.bfloat16, jnp.float32
    own, window = GROUP * rows, (GROUP + REACH) * rows
    vmem = pl.BlockSpec(memory_space=pltpu.VMEM)
    dma = pltpu.SemaphoreType.DMA
    qh, gh, kw, vw, dh = pl.pallas_call(
        spread_kernel,
        out_shape=(
            jax.ShapeDtypeStruct((own, DH), bf16),
            jax.ShapeDtypeStruct((own, DH), bf16),
            jax.ShapeDtypeStruct((window, DH), bf16),
            jax.ShapeDtypeStruct((window, DH), bf16),
            jax.ShapeDtypeStruct((GROUP, 8, rows), f32),
        ),
        in_specs=[vmem] * 5,
        out_specs=[vmem] * 5,
        scratch_shapes=[
            pltpu.VMEM((HEADS, 8, rows), f32),
            dma((5, GROUP)),
            dma((5, GROUP)),
            dma((2, GROUP)),
            dma((2, GROUP)),
            dma((5,)),
        ],
        compiler_params=pltpu.CompilerParams(
            collective_id=0, has_side_effects=True, vmem_limit_bytes=40 << 20
        ),
        name="spread",
    )(query_rows, key_rows, value_rows, forward_out, out_grad)
    dq, dk, dv, hk, hv = pl.pallas_call(
        grad_kernel,
        out_shape=(
            jax.ShapeDtypeStruct((own, DH), bf16),
            jax.ShapeDtypeStruct((own, DH), f32),
            jax.ShapeDtypeStruct((own, DH), f32),
            jax.ShapeDtypeStruct((window - own, DH), bf16),
            jax.ShapeDtypeStruct((window - own, DH), bf16),
        ),
        in_specs=[pl.BlockSpec(memory_space=pltpu.SMEM)] + [vmem] * 5,
        out_specs=[vmem] * 5,
        scratch_shapes=[
            pltpu.VMEM((window, DH), f32),
            pltpu.VMEM((window, DH), f32),
            pltpu.VMEM((GROUP, rows, rows), f32),
        ],
        compiler_params=pltpu.CompilerParams(vmem_limit_bytes=40 << 20),
        name="grad",
    )(doc_blocks, qh, gh, kw, vw, dh)
    return pl.pallas_call(
        collect_kernel,
        out_shape=(jax.ShapeDtypeStruct((rows, features), bf16),) * 3,
        in_specs=[vmem] * 5,
        out_specs=[vmem] * 3,
        scratch_shapes=[
            pltpu.VMEM((window - own, DH), bf16),
            pltpu.VMEM((window - own, DH), bf16),
            pltpu.VMEM((own, DH), bf16),
            pltpu.VMEM((own, DH), bf16),
            dma((3, GROUP)),
            dma((3, GROUP)),
            dma((2, GROUP)),
            dma((2, GROUP)),
            dma((3,)),
        ],
        compiler_params=pltpu.CompilerParams(
            collective_id=1, has_side_effects=True, vmem_limit_bytes=40 << 20
        ),
        name="collect",
    )(dq, dk, dv, hk, hv)


def solution(mesh):
    rows = P(("cx", "cy"), None)
    return jax.shard_map(
        per_device,
        mesh=mesh,
        in_specs=(rows, rows, rows, rows, rows, P()),
        out_specs=(rows, rows, rows),
        check_vma=False,
    )
```

```python
import math

import jax
import jax.numpy as jnp
from jax import lax
from jax.experimental import pallas as pl
from jax.experimental.pallas import tpu as pltpu
from jax.sharding import PartitionSpec as P

HEADS = 8
DH = 128
BLOCK = 128
REACH = 7
GROUP = 8
WIDE = 2
EXP2_SCALE = math.log2(math.e) / math.sqrt(DH)
MESH = pl.DeviceIdType.MESH
NT = (((1,), (1,)), ((), ()))
TN = (((0,), (0,)), ((), ()))


def place():
    inner = lax.axis_size("cy")
    count = lax.axis_size("cx") * inner
    shard = lax.axis_index("cx") * inner + lax.axis_index("cy")

    def device(index):
        return (index // inner, lax.rem(index, inner))

    return count, shard, device


def rows_at(index, rows):
    return pl.ds(pl.multiple_of(index * rows, rows), rows)


def cols_at(head):
    return pl.ds(pl.multiple_of(head * DH, DH), DH)


def spread_kernel(
    docs, q_ref, k_ref, v_ref, o_ref, g_ref, qh, gh, kw, vw, dh, lh,
    o_here, g_here, dsend, send, recv, fsend, frecv, local
):
    rows = q_ref.shape[0]
    count, shard, device = place()
    me = lax.rem(shard, GROUP)
    base = shard - me
    ahead = device(lax.rem(shard + GROUP, count))
    behind = device(lax.rem(shard + count - GROUP, count))
    tensors = ((k_ref, kw, REACH), (v_ref, vw, REACH), (q_ref, qh, 0), (g_ref, gh, 0))
    K, V, Q, G, DELTA = range(5)

    def out_copy(which, j):
        src, dst, shift = tensors[which]
        peer = lax.rem(me + j, GROUP)
        return pltpu.make_async_remote_copy(
            src_ref=src.at[:, cols_at(peer)],
            dst_ref=dst.at[rows_at(me + shift, rows), :],
            send_sem=send.at[which, j],
            recv_sem=recv.at[which, j],
            device_id=device(base + peer),
            device_id_type=MESH,
        )

    def in_copy(which, j):
        src, dst, shift = tensors[which]
        peer = lax.rem(me + GROUP - j, GROUP)
        return pltpu.make_async_remote_copy(
            src_ref=src.at[:, cols_at(peer)],
            dst_ref=dst.at[rows_at(peer + shift, rows), :],
            send_sem=send.at[which, j],
            recv_sem=recv.at[which, j],
            device_id=device(base + peer),
            device_id_type=MESH,
        )

    def own_copy(which):
        src, dst, shift = tensors[which]
        return pltpu.make_async_copy(
            src.at[:, cols_at(me)], dst.at[rows_at(me + shift, rows), :], local.at[which]
        )

    def forward(which, shard_in_group):
        _, dst, shift = tensors[which]
        return pltpu.make_async_remote_copy(
            src_ref=dst.at[rows_at(shard_in_group + shift, rows), :],
            dst_ref=dst.at[rows_at(shard_in_group - 1, rows), :],
            send_sem=fsend.at[which, shard_in_group],
            recv_sem=frecv.at[which, shard_in_group],
            device_id=ahead,
            device_id_type=MESH,
        )

    def forward_all(which):
        own_copy(which).wait()

        @pl.when(me >= 1)
        def _():
            forward(which, me).start()

        for j in range(1, GROUP):
            source = lax.rem(me + GROUP - j, GROUP)
            in_copy(which, j).wait_recv()

            @pl.when(source >= 1)
            def _():
                forward(which, source).start()

    g_copy = pltpu.make_async_copy(g_ref, g_here, local.at[5])
    o_copy = pltpu.make_async_copy(o_ref, o_here, local.at[6])
    barrier = pltpu.get_barrier_semaphore()
    for j in range(1, GROUP):
        peer = device(base + lax.rem(me + j, GROUP))
        pl.semaphore_signal(barrier, inc=1, device_id=peer, device_id_type=MESH)
    pl.semaphore_signal(barrier, inc=1, device_id=behind, device_id_type=MESH)
    for which in range(4):
        own_copy(which).start()
    g_copy.start()
    o_copy.start()
    pl.semaphore_wait(barrier, GROUP)

    for which in (K, Q):
        for j in range(1, GROUP):
            out_copy(which, j).start()

    g_copy.wait()
    o_copy.wait()
    ones = jnp.ones((8, DH), jnp.bfloat16)
    for head in range(HEADS):
        cols = slice(head * DH, (head + 1) * DH)
        product = g_here[:, cols].astype(jnp.float32) * o_here[:, cols].astype(jnp.float32)
        high = product.astype(jnp.bfloat16)
        low = (product - high.astype(jnp.float32)).astype(jnp.bfloat16)
        dsend[head] = lax.dot_general(
            ones, high, NT, preferred_element_type=jnp.float32
        ) + lax.dot_general(ones, low, NT, preferred_element_type=jnp.float32)

    def delta_copy(j, peer, source):
        return pltpu.make_async_remote_copy(
            src_ref=dsend.at[peer],
            dst_ref=dh.at[source],
            send_sem=send.at[DELTA, j],
            recv_sem=recv.at[DELTA, j],
            device_id=device(base + peer),
            device_id_type=MESH,
        )

    own_delta = pltpu.make_async_copy(dsend.at[me], dh.at[me], local.at[DELTA])
    own_delta.start()
    for j in range(1, GROUP):
        delta_copy(j, lax.rem(me + j, GROUP), me).start()

    forward_all(K)
    for which in (V, G):
        for j in range(1, GROUP):
            out_copy(which, j).start()
    own_copy(Q).wait()
    for j in range(1, GROUP):
        in_copy(Q, j).wait_recv()
    for s in range(1, GROUP):
        forward(K, s).wait_recv()

    masked = mask_maker(docs, base, rows)

    def stats(i, _):
        _, allowed = masked(i)
        q = qh[rows_at(i, rows), :]
        top = jnp.full((1, rows), -1e30, jnp.float32)
        total = jnp.zeros((1, rows), jnp.float32)
        for c in range((REACH + 1) // WIDE):
            j = i + c * WIDE
            s = lax.dot_general(
                kw[wide_at(j, rows), :], q, NT, preferred_element_type=jnp.float32
            )
            s = jnp.where(allowed(j), s * EXP2_SCALE, -1e30)
            higher = jnp.maximum(top, jnp.max(s, axis=0, keepdims=True))
            total = total * jnp.exp2(top - higher) + jnp.sum(
                jnp.exp2(s - higher), axis=0, keepdims=True
            )
            top = higher
        lh[i] = jnp.broadcast_to(top + jnp.log2(total), (8, rows))
        return 0

    lax.fori_loop(0, GROUP, stats, 0)
    forward_all(V)
    own_copy(G).wait()
    for j in range(1, GROUP):
        in_copy(G, j).wait_recv()
    own_delta.wait()
    for j in range(1, GROUP):
        peer = lax.rem(me + GROUP - j, GROUP)
        delta_copy(j, peer, peer).wait_recv()
    for s in range(1, GROUP):
        forward(V, s).wait_recv()
    for s in range(1, GROUP):
        for which in (K, V):
            forward(which, s).wait_send()
    for j in range(1, GROUP):
        for which in range(4):
            out_copy(which, j).wait_send()
        delta_copy(j, lax.rem(me + j, GROUP), me).wait_send()


def mask_maker(docs, base, rows):
    per_tile = rows // BLOCK
    group_block = base * per_tile
    key_at = lax.broadcasted_iota(jnp.int32, (WIDE * rows, rows), 0)
    lane = lax.broadcasted_iota(jnp.int32, (1, rows), 1)

    def masked(i):
        first_block = group_block + i * per_tile

        def look(n, state):
            start, firsts = state
            firsts = tuple(
                jnp.where(start <= first_block + b, start, firsts[b]) for b in range(per_tile)
            )
            return start + docs[n], firsts

        _, firsts = lax.fori_loop(
            0,
            docs.shape[0],
            look,
            (jnp.int32(0), tuple(jnp.int32(0) for _ in range(per_tile))),
        )
        firsts = [f - group_block + REACH * per_tile for f in firsts]
        start_row = jnp.full((1, rows), 0, jnp.int32)
        for b in range(per_tile):
            start_row = jnp.where(lane >= b * BLOCK, firsts[b] * BLOCK, start_row)
        last_row = (i + REACH) * rows + lane

        def allowed(j):
            return (key_at >= start_row - j * rows) & (key_at <= last_row - j * rows)

        return firsts[0] // per_tile, allowed

    return masked


def wide_at(j, rows):
    return pl.ds(pl.multiple_of(j * rows, rows), WIDE * rows)


def grad_kernel(
    docs, q_ref, g_ref, k_ref, v_ref, d_ref, l_ref, dq_ref, dk_ref, dv_ref, hk_ref, hv_ref, dk, dv
):
    rows = q_ref.shape[0] // GROUP
    scale = 1.0 / math.sqrt(DH)
    _, shard, _ = place()
    dk[...] = jnp.zeros_like(dk)
    dv[...] = jnp.zeros_like(dv)
    masked = mask_maker(docs, shard - lax.rem(shard, GROUP), rows)

    def tile(i, _):
        begin, allowed = masked(i)
        end = i + REACH + 1
        steps = (end - begin + WIDE - 1) // WIDE
        q = q_ref[rows_at(i, rows), :]
        g = g_ref[rows_at(i, rows), :]
        delta = d_ref[i, 0:1, :]
        logsum = l_ref[i, 0:1, :]

        def grads(c, dq):
            j = end - (c + 1) * WIDE
            at = wide_at(j, rows)
            k = k_ref[at, :]
            s = lax.dot_general(k, q, NT, preferred_element_type=jnp.float32)
            dprob = lax.dot_general(v_ref[at, :], g, NT, preferred_element_type=jnp.float32)
            prob = jnp.exp2(jnp.where(allowed(j), s * EXP2_SCALE - logsum, -1e30))
            ds = (prob * (dprob - delta)).astype(jnp.bfloat16)
            dv[at, :] += jnp.dot(prob.astype(jnp.bfloat16), g, preferred_element_type=jnp.float32)
            dk[at, :] += jnp.dot(ds, q, preferred_element_type=jnp.float32)
            return dq + lax.dot_general(ds, k, TN, preferred_element_type=jnp.float32)

        dq = lax.fori_loop(0, steps, grads, jnp.zeros((rows, DH), jnp.float32))
        dq_ref[rows_at(i, rows), :] = (dq * scale).astype(jnp.bfloat16)
        return 0

    lax.fori_loop(0, GROUP, tile, 0)
    halo = REACH * rows
    hk_ref[...] = (dk[:halo, :] * scale).astype(jnp.bfloat16)
    hv_ref[...] = dv[:halo, :].astype(jnp.bfloat16)
    dk_ref[...] = dk[halo:, :] * scale
    dv_ref[...] = dv[halo:, :]


def collect_kernel(
    dq_ref, dk_ref, dv_ref, hk_ref, hv_ref, qo, ko, vo, hk, hv, ks, vs, send, recv, hsend, hrecv, local
):
    rows = qo.shape[0]
    count, shard, device = place()
    me = lax.rem(shard, GROUP)
    base = shard - me
    ahead = device(lax.rem(shard + GROUP, count))
    behind = device(lax.rem(shard + count - GROUP, count))
    barrier = pltpu.get_barrier_semaphore()
    for j in range(1, GROUP):
        peer = device(base + lax.rem(me + j, GROUP))
        pl.semaphore_signal(barrier, inc=1, device_id=peer, device_id_type=MESH)
    pl.semaphore_signal(barrier, inc=1, device_id=ahead, device_id_type=MESH)
    pl.semaphore_wait(barrier, GROUP)

    halos = ((hk_ref, hk), (hv_ref, hv))

    def halo_copy(which, s):
        src, dst = halos[which]
        at = rows_at(s - 1, rows)
        return pltpu.make_async_remote_copy(
            src_ref=src.at[at, :],
            dst_ref=dst.at[at, :],
            send_sem=hsend.at[which, s],
            recv_sem=hrecv.at[which, s],
            device_id=behind,
            device_id_type=MESH,
        )

    tensors = ((dq_ref, qo), (ks, ko), (vs, vo))

    def out_copy(which, j):
        src, dst = tensors[which]
        peer = lax.rem(me + j, GROUP)
        return pltpu.make_async_remote_copy(
            src_ref=src.at[rows_at(peer, rows), :],
            dst_ref=dst.at[:, cols_at(me)],
            send_sem=send.at[which, j],
            recv_sem=recv.at[which, j],
            device_id=device(base + peer),
            device_id_type=MESH,
        )

    def in_copy(which, j):
        src, dst = tensors[which]
        peer = lax.rem(me + GROUP - j, GROUP)
        return pltpu.make_async_remote_copy(
            src_ref=src.at[rows_at(peer, rows), :],
            dst_ref=dst.at[:, cols_at(peer)],
            send_sem=send.at[which, j],
            recv_sem=recv.at[which, j],
            device_id=device(base + peer),
            device_id_type=MESH,
        )

    def own_copy(which):
        src, dst = tensors[which]
        return pltpu.make_async_copy(
            src.at[rows_at(me, rows), :], dst.at[:, cols_at(me)], local.at[which]
        )

    for j in range(GROUP):
        s = lax.rem(me + j, GROUP)

        @pl.when(s >= 1)
        def _():
            for which in range(2):
                halo_copy(which, s).start()

    own_copy(0).start()
    for j in range(1, GROUP):
        out_copy(0, j).start()

    for j in [*range(1, GROUP), 0]:
        s = lax.rem(me + j, GROUP)
        at = rows_at(s, rows)

        @pl.when(s == 0)
        def _():
            ks[at, :] = dk_ref[at, :].astype(jnp.bfloat16)
            vs[at, :] = dv_ref[at, :].astype(jnp.bfloat16)

        @pl.when(s >= 1)
        def _():
            before = rows_at(s - 1, rows)
            halo_copy(0, s).wait_recv()
            ks[at, :] = (dk_ref[at, :] + hk[before, :].astype(jnp.float32)).astype(jnp.bfloat16)
            halo_copy(1, s).wait_recv()
            vs[at, :] = (dv_ref[at, :] + hv[before, :].astype(jnp.float32)).astype(jnp.bfloat16)

        for which in (1, 2):
            if j:
                out_copy(which, j).start()
            else:
                own_copy(which).start()

    for which in range(3):
        own_copy(which).wait()
        for j in range(1, GROUP):
            in_copy(which, j).wait_recv()
    for which in range(3):
        for j in range(1, GROUP):
            out_copy(which, j).wait_send()
    for s in range(1, GROUP):
        for which in range(2):
            halo_copy(which, s).wait_send()


def per_device(query_rows, key_rows, value_rows, forward_out, out_grad, doc_blocks):
    rows, features = query_rows.shape
    bf16, f32 = jnp.bfloat16, jnp.float32
    own, window = GROUP * rows, (GROUP + REACH) * rows
    vmem = pl.BlockSpec(memory_space=pltpu.VMEM)
    dma = pltpu.SemaphoreType.DMA
    smem = pl.BlockSpec(memory_space=pltpu.SMEM)
    hbm = pl.BlockSpec(memory_space=pltpu.HBM)
    qh, gh, kw, vw, dh, lh = pl.pallas_call(
        spread_kernel,
        out_shape=(
            jax.ShapeDtypeStruct((own, DH), bf16),
            jax.ShapeDtypeStruct((own, DH), bf16),
            jax.ShapeDtypeStruct((window, DH), bf16),
            jax.ShapeDtypeStruct((window, DH), bf16),
            jax.ShapeDtypeStruct((GROUP, 8, rows), f32),
            jax.ShapeDtypeStruct((GROUP, 8, rows), f32),
        ),
        in_specs=[smem] + [hbm] * 5,
        out_specs=[vmem] * 6,
        scratch_shapes=[
            pltpu.VMEM((rows, features), bf16),
            pltpu.VMEM((rows, features), bf16),
            pltpu.VMEM((HEADS, 8, rows), f32),
            dma((5, GROUP)),
            dma((5, GROUP)),
            dma((2, GROUP)),
            dma((2, GROUP)),
            dma((7,)),
        ],
        compiler_params=pltpu.CompilerParams(
            collective_id=0, has_side_effects=True, vmem_limit_bytes=40 << 20
        ),
        name="spread",
    )(doc_blocks, query_rows, key_rows, value_rows, forward_out, out_grad)
    dq, dk, dv, hk, hv = pl.pallas_call(
        grad_kernel,
        out_shape=(
            jax.ShapeDtypeStruct((own, DH), bf16),
            jax.ShapeDtypeStruct((own, DH), f32),
            jax.ShapeDtypeStruct((own, DH), f32),
            jax.ShapeDtypeStruct((window - own, DH), bf16),
            jax.ShapeDtypeStruct((window - own, DH), bf16),
        ),
        in_specs=[smem] + [vmem] * 6,
        out_specs=[vmem] * 5,
        scratch_shapes=[
            pltpu.VMEM((window, DH), f32),
            pltpu.VMEM((window, DH), f32),
        ],
        compiler_params=pltpu.CompilerParams(vmem_limit_bytes=40 << 20),
        name="grad",
    )(doc_blocks, qh, gh, kw, vw, dh, lh)
    return pl.pallas_call(
        collect_kernel,
        out_shape=(jax.ShapeDtypeStruct((rows, features), bf16),) * 3,
        in_specs=[vmem] * 5,
        out_specs=[vmem] * 3,
        scratch_shapes=[
            pltpu.VMEM((window - own, DH), bf16),
            pltpu.VMEM((window - own, DH), bf16),
            pltpu.VMEM((own, DH), bf16),
            pltpu.VMEM((own, DH), bf16),
            dma((3, GROUP)),
            dma((3, GROUP)),
            dma((2, GROUP)),
            dma((2, GROUP)),
            dma((3,)),
        ],
        compiler_params=pltpu.CompilerParams(
            collective_id=1, has_side_effects=True, vmem_limit_bytes=40 << 20
        ),
        name="collect",
    )(dq, dk, dv, hk, hv)


def solution(mesh):
    rows = P(("cx", "cy"), None)
    return jax.shard_map(
        per_device,
        mesh=mesh,
        in_specs=(rows, rows, rows, rows, rows, P()),
        out_specs=(rows, rows, rows),
        check_vma=False,
    )
```

```python
import math

import jax
import jax.numpy as jnp
from jax import lax
from jax.experimental import pallas as pl
from jax.experimental.pallas import tpu as pltpu
from jax.sharding import PartitionSpec as P

HEADS = 8
DH = 128
BLOCK = 128
REACH = 7
GROUP = 8
WIDE = 2
EXP2_SCALE = math.log2(math.e) / math.sqrt(DH)
MESH = pl.DeviceIdType.MESH
NT = (((1,), (1,)), ((), ()))
TN = (((0,), (0,)), ((), ()))


def place():
    inner = lax.axis_size("cy")
    count = lax.axis_size("cx") * inner
    shard = lax.axis_index("cx") * inner + lax.axis_index("cy")

    def device(index):
        return (index // inner, lax.rem(index, inner))

    return count, shard, device


def rows_at(index, rows):
    return pl.ds(pl.multiple_of(index * rows, rows), rows)


def cols_at(head):
    return pl.ds(pl.multiple_of(head * DH, DH), DH)


def spread_kernel(
    docs, q_ref, k_ref, v_ref, o_ref, g_ref, qh, gh, kw, vw, dh, lh,
    o_here, g_here, dsend, send, recv, fsend, frecv, local
):
    rows = q_ref.shape[0]
    count, shard, device = place()
    me = lax.rem(shard, GROUP)
    base = shard - me
    ahead = device(lax.rem(shard + GROUP, count))
    behind = device(lax.rem(shard + count - GROUP, count))
    tensors = ((k_ref, kw, REACH), (v_ref, vw, REACH), (q_ref, qh, 0), (g_ref, gh, 0))
    K, V, Q, G, DELTA = range(5)

    def out_copy(which, j):
        src, dst, shift = tensors[which]
        peer = lax.rem(me + j, GROUP)
        return pltpu.make_async_remote_copy(
            src_ref=src.at[:, cols_at(peer)],
            dst_ref=dst.at[rows_at(me + shift, rows), :],
            send_sem=send.at[which, j],
            recv_sem=recv.at[which, j],
            device_id=device(base + peer),
            device_id_type=MESH,
        )

    def in_copy(which, j):
        src, dst, shift = tensors[which]
        peer = lax.rem(me + GROUP - j, GROUP)
        return pltpu.make_async_remote_copy(
            src_ref=src.at[:, cols_at(peer)],
            dst_ref=dst.at[rows_at(peer + shift, rows), :],
            send_sem=send.at[which, j],
            recv_sem=recv.at[which, j],
            device_id=device(base + peer),
            device_id_type=MESH,
        )

    def own_copy(which):
        src, dst, shift = tensors[which]
        return pltpu.make_async_copy(
            src.at[:, cols_at(me)], dst.at[rows_at(me + shift, rows), :], local.at[which]
        )

    def forward(which, shard_in_group):
        _, dst, shift = tensors[which]
        return pltpu.make_async_remote_copy(
            src_ref=dst.at[rows_at(shard_in_group + shift, rows), :],
            dst_ref=dst.at[rows_at(shard_in_group - 1, rows), :],
            send_sem=fsend.at[which, shard_in_group],
            recv_sem=frecv.at[which, shard_in_group],
            device_id=ahead,
            device_id_type=MESH,
        )

    def forward_all(which):
        own_copy(which).wait()

        @pl.when(me >= 1)
        def _():
            forward(which, me).start()

        for j in range(1, GROUP):
            source = lax.rem(me + GROUP - j, GROUP)
            in_copy(which, j).wait_recv()

            @pl.when(source >= 1)
            def _():
                forward(which, source).start()

    g_copy = pltpu.make_async_copy(g_ref, g_here, local.at[5])
    o_copy = pltpu.make_async_copy(o_ref, o_here, local.at[6])
    barrier = pltpu.get_barrier_semaphore()
    for j in range(1, GROUP):
        peer = device(base + lax.rem(me + j, GROUP))
        pl.semaphore_signal(barrier, inc=1, device_id=peer, device_id_type=MESH)
    pl.semaphore_signal(barrier, inc=1, device_id=behind, device_id_type=MESH)
    for which in range(4):
        own_copy(which).start()
    g_copy.start()
    o_copy.start()
    pl.semaphore_wait(barrier, GROUP)

    for which in (K, V):
        for j in range(1, GROUP):
            out_copy(which, j).start()

    g_copy.wait()
    o_copy.wait()
    ones = jnp.ones((8, DH), jnp.bfloat16)
    for head in range(HEADS):
        cols = slice(head * DH, (head + 1) * DH)
        product = g_here[:, cols].astype(jnp.float32) * o_here[:, cols].astype(jnp.float32)
        high = product.astype(jnp.bfloat16)
        low = (product - high.astype(jnp.float32)).astype(jnp.bfloat16)
        dsend[head] = lax.dot_general(
            ones, high, NT, preferred_element_type=jnp.float32
        ) + lax.dot_general(ones, low, NT, preferred_element_type=jnp.float32)

    def delta_copy(j, peer, source):
        return pltpu.make_async_remote_copy(
            src_ref=dsend.at[peer],
            dst_ref=dh.at[source],
            send_sem=send.at[DELTA, j],
            recv_sem=recv.at[DELTA, j],
            device_id=device(base + peer),
            device_id_type=MESH,
        )

    own_delta = pltpu.make_async_copy(dsend.at[me], dh.at[me], local.at[DELTA])
    own_delta.start()
    for j in range(1, GROUP):
        delta_copy(j, lax.rem(me + j, GROUP), me).start()

    forward_all(K)
    for j in range(1, GROUP):
        out_copy(Q, j).start()
    forward_all(V)
    for j in range(1, GROUP):
        out_copy(G, j).start()
    own_copy(Q).wait()
    for j in range(1, GROUP):
        in_copy(Q, j).wait_recv()
    for s in range(1, GROUP):
        forward(K, s).wait_recv()

    masked = mask_maker(docs, base, rows)

    def stats(i, _):
        _, allowed = masked(i)
        q = qh[rows_at(i, rows), :]
        top = jnp.full((1, rows), -1e30, jnp.float32)
        total = jnp.zeros((1, rows), jnp.float32)
        for c in range((REACH + 1) // WIDE):
            j = i + c * WIDE
            s = lax.dot_general(
                kw[wide_at(j, rows), :], q, NT, preferred_element_type=jnp.float32
            )
            s = jnp.where(allowed(j), s * EXP2_SCALE, -1e30)
            higher = jnp.maximum(top, jnp.max(s, axis=0, keepdims=True))
            total = total * jnp.exp2(top - higher) + jnp.sum(
                jnp.exp2(s - higher), axis=0, keepdims=True
            )
            top = higher
        lh[i] = jnp.broadcast_to(top + jnp.log2(total), (8, rows))
        return 0

    lax.fori_loop(0, GROUP, stats, 0)
    own_copy(G).wait()
    for j in range(1, GROUP):
        in_copy(G, j).wait_recv()
    own_delta.wait()
    for j in range(1, GROUP):
        peer = lax.rem(me + GROUP - j, GROUP)
        delta_copy(j, peer, peer).wait_recv()
    for s in range(1, GROUP):
        forward(V, s).wait_recv()
    for s in range(1, GROUP):
        for which in (K, V):
            forward(which, s).wait_send()
    for j in range(1, GROUP):
        for which in range(4):
            out_copy(which, j).wait_send()
        delta_copy(j, lax.rem(me + j, GROUP), me).wait_send()


def mask_maker(docs, base, rows):
    per_tile = rows // BLOCK
    group_block = base * per_tile
    key_at = lax.broadcasted_iota(jnp.int32, (WIDE * rows, rows), 0)
    lane = lax.broadcasted_iota(jnp.int32, (1, rows), 1)

    def masked(i):
        first_block = group_block + i * per_tile

        def look(n, state):
            start, firsts = state
            firsts = tuple(
                jnp.where(start <= first_block + b, start, firsts[b]) for b in range(per_tile)
            )
            return start + docs[n], firsts

        _, firsts = lax.fori_loop(
            0,
            docs.shape[0],
            look,
            (jnp.int32(0), tuple(jnp.int32(0) for _ in range(per_tile))),
        )
        firsts = [f - group_block + REACH * per_tile for f in firsts]
        start_row = jnp.full((1, rows), 0, jnp.int32)
        for b in range(per_tile):
            start_row = jnp.where(lane >= b * BLOCK, firsts[b] * BLOCK, start_row)
        last_row = (i + REACH) * rows + lane

        def allowed(j):
            return (key_at >= start_row - j * rows) & (key_at <= last_row - j * rows)

        return firsts[0] // per_tile, allowed

    return masked


def wide_at(j, rows):
    return pl.ds(pl.multiple_of(j * rows, rows), WIDE * rows)


def grad_kernel(
    docs, q_ref, g_ref, k_ref, v_ref, d_ref, l_ref, dq_ref, dk_ref, dv_ref, hk_ref, hv_ref, dk, dv
):
    rows = q_ref.shape[0] // GROUP
    scale = 1.0 / math.sqrt(DH)
    _, shard, _ = place()
    dk[...] = jnp.zeros_like(dk)
    dv[...] = jnp.zeros_like(dv)
    masked = mask_maker(docs, shard - lax.rem(shard, GROUP), rows)

    def tile(i, _):
        begin, allowed = masked(i)
        end = i + REACH + 1
        steps = (end - begin + WIDE - 1) // WIDE
        q = q_ref[rows_at(i, rows), :]
        g = g_ref[rows_at(i, rows), :]
        delta = d_ref[i, 0:1, :]
        logsum = l_ref[i, 0:1, :]

        def grads(c, dq):
            j = end - (c + 1) * WIDE
            at = wide_at(j, rows)
            k = k_ref[at, :]
            s = lax.dot_general(k, q, NT, preferred_element_type=jnp.float32)
            dprob = lax.dot_general(v_ref[at, :], g, NT, preferred_element_type=jnp.float32)
            prob = jnp.exp2(jnp.where(allowed(j), s * EXP2_SCALE - logsum, -1e30))
            ds = (prob * (dprob - delta)).astype(jnp.bfloat16)
            dv[at, :] += jnp.dot(prob.astype(jnp.bfloat16), g, preferred_element_type=jnp.float32)
            dk[at, :] += jnp.dot(ds, q, preferred_element_type=jnp.float32)
            return dq + lax.dot_general(ds, k, TN, preferred_element_type=jnp.float32)

        dq = lax.fori_loop(0, steps, grads, jnp.zeros((rows, DH), jnp.float32))
        dq_ref[rows_at(i, rows), :] = (dq * scale).astype(jnp.bfloat16)
        return 0

    lax.fori_loop(0, GROUP, tile, 0)
    halo = REACH * rows
    hk_ref[...] = (dk[:halo, :] * scale).astype(jnp.bfloat16)
    hv_ref[...] = dv[:halo, :].astype(jnp.bfloat16)
    dk_ref[...] = dk[halo:, :] * scale
    dv_ref[...] = dv[halo:, :]


def collect_kernel(
    dq_ref, dk_ref, dv_ref, hk_ref, hv_ref, qo, ko, vo, hk, hv, ks, vs, send, recv, hsend, hrecv, local
):
    rows = qo.shape[0]
    count, shard, device = place()
    me = lax.rem(shard, GROUP)
    base = shard - me
    ahead = device(lax.rem(shard + GROUP, count))
    behind = device(lax.rem(shard + count - GROUP, count))
    barrier = pltpu.get_barrier_semaphore()
    for j in range(1, GROUP):
        peer = device(base + lax.rem(me + j, GROUP))
        pl.semaphore_signal(barrier, inc=1, device_id=peer, device_id_type=MESH)
    pl.semaphore_signal(barrier, inc=1, device_id=ahead, device_id_type=MESH)
    pl.semaphore_wait(barrier, GROUP)

    halos = ((hk_ref, hk), (hv_ref, hv))

    def halo_copy(which, s):
        src, dst = halos[which]
        at = rows_at(s - 1, rows)
        return pltpu.make_async_remote_copy(
            src_ref=src.at[at, :],
            dst_ref=dst.at[at, :],
            send_sem=hsend.at[which, s],
            recv_sem=hrecv.at[which, s],
            device_id=behind,
            device_id_type=MESH,
        )

    tensors = ((dq_ref, qo), (ks, ko), (vs, vo))

    def out_copy(which, j):
        src, dst = tensors[which]
        peer = lax.rem(me + j, GROUP)
        return pltpu.make_async_remote_copy(
            src_ref=src.at[rows_at(peer, rows), :],
            dst_ref=dst.at[:, cols_at(me)],
            send_sem=send.at[which, j],
            recv_sem=recv.at[which, j],
            device_id=device(base + peer),
            device_id_type=MESH,
        )

    def in_copy(which, j):
        src, dst = tensors[which]
        peer = lax.rem(me + GROUP - j, GROUP)
        return pltpu.make_async_remote_copy(
            src_ref=src.at[rows_at(peer, rows), :],
            dst_ref=dst.at[:, cols_at(peer)],
            send_sem=send.at[which, j],
            recv_sem=recv.at[which, j],
            device_id=device(base + peer),
            device_id_type=MESH,
        )

    def own_copy(which):
        src, dst = tensors[which]
        return pltpu.make_async_copy(
            src.at[rows_at(me, rows), :], dst.at[:, cols_at(me)], local.at[which]
        )

    for j in range(GROUP):
        s = lax.rem(me + j, GROUP)

        @pl.when(s >= 1)
        def _():
            for which in range(2):
                halo_copy(which, s).start()

    own_copy(0).start()
    for j in range(1, GROUP):
        out_copy(0, j).start()

    for j in [*range(1, GROUP), 0]:
        s = lax.rem(me + j, GROUP)
        at = rows_at(s, rows)

        @pl.when(s == 0)
        def _():
            ks[at, :] = dk_ref[at, :].astype(jnp.bfloat16)
            vs[at, :] = dv_ref[at, :].astype(jnp.bfloat16)

        @pl.when(s >= 1)
        def _():
            before = rows_at(s - 1, rows)
            halo_copy(0, s).wait_recv()
            ks[at, :] = (dk_ref[at, :] + hk[before, :].astype(jnp.float32)).astype(jnp.bfloat16)
            halo_copy(1, s).wait_recv()
            vs[at, :] = (dv_ref[at, :] + hv[before, :].astype(jnp.float32)).astype(jnp.bfloat16)

        for which in (1, 2):
            if j:
                out_copy(which, j).start()
            else:
                own_copy(which).start()

    for which in range(3):
        own_copy(which).wait()
        for j in range(1, GROUP):
            in_copy(which, j).wait_recv()
    for which in range(3):
        for j in range(1, GROUP):
            out_copy(which, j).wait_send()
    for s in range(1, GROUP):
        for which in range(2):
            halo_copy(which, s).wait_send()


def per_device(query_rows, key_rows, value_rows, forward_out, out_grad, doc_blocks):
    rows, features = query_rows.shape
    bf16, f32 = jnp.bfloat16, jnp.float32
    own, window = GROUP * rows, (GROUP + REACH) * rows
    vmem = pl.BlockSpec(memory_space=pltpu.VMEM)
    dma = pltpu.SemaphoreType.DMA
    smem = pl.BlockSpec(memory_space=pltpu.SMEM)
    hbm = pl.BlockSpec(memory_space=pltpu.HBM)
    qh, gh, kw, vw, dh, lh = pl.pallas_call(
        spread_kernel,
        out_shape=(
            jax.ShapeDtypeStruct((own, DH), bf16),
            jax.ShapeDtypeStruct((own, DH), bf16),
            jax.ShapeDtypeStruct((window, DH), bf16),
            jax.ShapeDtypeStruct((window, DH), bf16),
            jax.ShapeDtypeStruct((GROUP, 8, rows), f32),
            jax.ShapeDtypeStruct((GROUP, 8, rows), f32),
        ),
        in_specs=[smem] + [hbm] * 5,
        out_specs=[vmem] * 6,
        scratch_shapes=[
            pltpu.VMEM((rows, features), bf16),
            pltpu.VMEM((rows, features), bf16),
            pltpu.VMEM((HEADS, 8, rows), f32),
            dma((5, GROUP)),
            dma((5, GROUP)),
            dma((2, GROUP)),
            dma((2, GROUP)),
            dma((7,)),
        ],
        compiler_params=pltpu.CompilerParams(
            collective_id=0, has_side_effects=True, vmem_limit_bytes=40 << 20
        ),
        name="spread",
    )(doc_blocks, query_rows, key_rows, value_rows, forward_out, out_grad)
    dq, dk, dv, hk, hv = pl.pallas_call(
        grad_kernel,
        out_shape=(
            jax.ShapeDtypeStruct((own, DH), bf16),
            jax.ShapeDtypeStruct((own, DH), f32),
            jax.ShapeDtypeStruct((own, DH), f32),
            jax.ShapeDtypeStruct((window - own, DH), bf16),
            jax.ShapeDtypeStruct((window - own, DH), bf16),
        ),
        in_specs=[smem] + [vmem] * 6,
        out_specs=[vmem] * 5,
        scratch_shapes=[
            pltpu.VMEM((window, DH), f32),
            pltpu.VMEM((window, DH), f32),
        ],
        compiler_params=pltpu.CompilerParams(vmem_limit_bytes=40 << 20),
        name="grad",
    )(doc_blocks, qh, gh, kw, vw, dh, lh)
    return pl.pallas_call(
        collect_kernel,
        out_shape=(jax.ShapeDtypeStruct((rows, features), bf16),) * 3,
        in_specs=[vmem] * 5,
        out_specs=[vmem] * 3,
        scratch_shapes=[
            pltpu.VMEM((window - own, DH), bf16),
            pltpu.VMEM((window - own, DH), bf16),
            pltpu.VMEM((own, DH), bf16),
            pltpu.VMEM((own, DH), bf16),
            dma((3, GROUP)),
            dma((3, GROUP)),
            dma((2, GROUP)),
            dma((2, GROUP)),
            dma((3,)),
        ],
        compiler_params=pltpu.CompilerParams(
            collective_id=1, has_side_effects=True, vmem_limit_bytes=40 << 20
        ),
        name="collect",
    )(dq, dk, dv, hk, hv)


def solution(mesh):
    rows = P(("cx", "cy"), None)
    return jax.shard_map(
        per_device,
        mesh=mesh,
        in_specs=(rows, rows, rows, rows, rows, P()),
        out_specs=(rows, rows, rows),
        check_vma=False,
    )
```

```python
import math

import jax
import jax.numpy as jnp
from jax import lax
from jax.experimental import pallas as pl
from jax.experimental.pallas import tpu as pltpu
from jax.sharding import PartitionSpec as P

HEADS = 8
DH = 128
BLOCK = 128
REACH = 7
GROUP = 8
WIDE = 2
EXP2_SCALE = math.log2(math.e) / math.sqrt(DH)
MESH = pl.DeviceIdType.MESH
NT = (((1,), (1,)), ((), ()))
TN = (((0,), (0,)), ((), ()))


def place():
    inner = lax.axis_size("cy")
    count = lax.axis_size("cx") * inner
    shard = lax.axis_index("cx") * inner + lax.axis_index("cy")

    def device(index):
        return (index // inner, lax.rem(index, inner))

    return count, shard, device


def rows_at(index, rows):
    return pl.ds(pl.multiple_of(index * rows, rows), rows)


def cols_at(head):
    return pl.ds(pl.multiple_of(head * DH, DH), DH)


def spread_kernel(
    docs, q_ref, k_ref, v_ref, o_ref, g_ref, qh, gh, kw, vw, dh, lh,
    o_here, g_here, dsend, send, recv, fsend, frecv, local
):
    rows = q_ref.shape[0]
    count, shard, device = place()
    me = lax.rem(shard, GROUP)
    base = shard - me
    ahead = device(lax.rem(shard + GROUP, count))
    behind = device(lax.rem(shard + count - GROUP, count))
    tensors = ((k_ref, kw, REACH), (v_ref, vw, REACH), (q_ref, qh, 0), (g_ref, gh, 0))
    K, V, Q, G, DELTA = range(5)

    def out_copy(which, j):
        src, dst, shift = tensors[which]
        peer = lax.rem(me + j, GROUP)
        return pltpu.make_async_remote_copy(
            src_ref=src.at[:, cols_at(peer)],
            dst_ref=dst.at[rows_at(me + shift, rows), :],
            send_sem=send.at[which, j],
            recv_sem=recv.at[which, j],
            device_id=device(base + peer),
            device_id_type=MESH,
        )

    def in_copy(which, j):
        src, dst, shift = tensors[which]
        peer = lax.rem(me + GROUP - j, GROUP)
        return pltpu.make_async_remote_copy(
            src_ref=src.at[:, cols_at(peer)],
            dst_ref=dst.at[rows_at(peer + shift, rows), :],
            send_sem=send.at[which, j],
            recv_sem=recv.at[which, j],
            device_id=device(base + peer),
            device_id_type=MESH,
        )

    def own_copy(which):
        src, dst, shift = tensors[which]
        return pltpu.make_async_copy(
            src.at[:, cols_at(me)], dst.at[rows_at(me + shift, rows), :], local.at[which]
        )

    def forward(which, shard_in_group):
        _, dst, shift = tensors[which]
        return pltpu.make_async_remote_copy(
            src_ref=dst.at[rows_at(shard_in_group + shift, rows), :],
            dst_ref=dst.at[rows_at(shard_in_group - 1, rows), :],
            send_sem=fsend.at[which, shard_in_group],
            recv_sem=frecv.at[which, shard_in_group],
            device_id=ahead,
            device_id_type=MESH,
        )

    def forward_own(which):
        own_copy(which).wait()

        @pl.when(me >= 1)
        def _():
            forward(which, me).start()

    def forward_from(which, j):
        source = lax.rem(me + GROUP - j, GROUP)
        in_copy(which, j).wait_recv()

        @pl.when(source >= 1)
        def _():
            forward(which, source).start()

    def forward_all(which):
        forward_own(which)
        for j in range(1, GROUP):
            forward_from(which, j)

    g_copy = pltpu.make_async_copy(g_ref, g_here, local.at[5])
    o_copy = pltpu.make_async_copy(o_ref, o_here, local.at[6])
    barrier = pltpu.get_barrier_semaphore()
    for j in range(1, GROUP):
        peer = device(base + lax.rem(me + j, GROUP))
        pl.semaphore_signal(barrier, inc=1, device_id=peer, device_id_type=MESH)
    pl.semaphore_signal(barrier, inc=1, device_id=behind, device_id_type=MESH)
    for which in range(4):
        own_copy(which).start()
    g_copy.start()
    o_copy.start()
    pl.semaphore_wait(barrier, GROUP)

    for which in (K, Q):
        for j in range(1, GROUP):
            out_copy(which, j).start()

    g_copy.wait()
    o_copy.wait()
    ones = jnp.ones((8, DH), jnp.bfloat16)
    for head in range(HEADS):
        cols = slice(head * DH, (head + 1) * DH)
        product = g_here[:, cols].astype(jnp.float32) * o_here[:, cols].astype(jnp.float32)
        high = product.astype(jnp.bfloat16)
        low = (product - high.astype(jnp.float32)).astype(jnp.bfloat16)
        dsend[head] = lax.dot_general(
            ones, high, NT, preferred_element_type=jnp.float32
        ) + lax.dot_general(ones, low, NT, preferred_element_type=jnp.float32)

    def delta_copy(j, peer, source):
        return pltpu.make_async_remote_copy(
            src_ref=dsend.at[peer],
            dst_ref=dh.at[source],
            send_sem=send.at[DELTA, j],
            recv_sem=recv.at[DELTA, j],
            device_id=device(base + peer),
            device_id_type=MESH,
        )

    own_delta = pltpu.make_async_copy(dsend.at[me], dh.at[me], local.at[DELTA])
    own_delta.start()
    for j in range(1, GROUP):
        delta_copy(j, lax.rem(me + j, GROUP), me).start()

    forward_all(K)
    for which in (V, G):
        for j in range(1, GROUP):
            out_copy(which, j).start()
    forward_own(V)
    own_copy(Q).wait()
    for j in range(1, GROUP):
        in_copy(Q, j).wait_recv()
    for s in range(1, GROUP):
        forward(K, s).wait_recv()

    masked = mask_maker(docs, base, rows)

    def stats(i, _):
        _, allowed = masked(i)
        q = qh[rows_at(i, rows), :]
        top = jnp.full((1, rows), -1e30, jnp.float32)
        total = jnp.zeros((1, rows), jnp.float32)
        for c in range((REACH + 1) // WIDE):
            j = i + c * WIDE
            s = lax.dot_general(
                kw[wide_at(j, rows), :], q, NT, preferred_element_type=jnp.float32
            )
            s = jnp.where(allowed(j), s * EXP2_SCALE, -1e30)
            higher = jnp.maximum(top, jnp.max(s, axis=0, keepdims=True))
            total = total * jnp.exp2(top - higher) + jnp.sum(
                jnp.exp2(s - higher), axis=0, keepdims=True
            )
            top = higher
        lh[i] = jnp.broadcast_to(top + jnp.log2(total), (8, rows))

        @pl.when(i >= 1)
        def _():
            forward_from(V, i)

        return 0

    lax.fori_loop(0, GROUP, stats, 0)
    own_copy(G).wait()
    for j in range(1, GROUP):
        in_copy(G, j).wait_recv()
    own_delta.wait()
    for j in range(1, GROUP):
        peer = lax.rem(me + GROUP - j, GROUP)
        delta_copy(j, peer, peer).wait_recv()
    for s in range(1, GROUP):
        forward(V, s).wait_recv()
    for s in range(1, GROUP):
        for which in (K, V):
            forward(which, s).wait_send()
    for j in range(1, GROUP):
        for which in range(4):
            out_copy(which, j).wait_send()
        delta_copy(j, lax.rem(me + j, GROUP), me).wait_send()


def mask_maker(docs, base, rows):
    per_tile = rows // BLOCK
    group_block = base * per_tile
    key_at = lax.broadcasted_iota(jnp.int32, (WIDE * rows, rows), 0)
    lane = lax.broadcasted_iota(jnp.int32, (1, rows), 1)

    def masked(i):
        first_block = group_block + i * per_tile

        def look(n, state):
            start, firsts = state
            firsts = tuple(
                jnp.where(start <= first_block + b, start, firsts[b]) for b in range(per_tile)
            )
            return start + docs[n], firsts

        _, firsts = lax.fori_loop(
            0,
            docs.shape[0],
            look,
            (jnp.int32(0), tuple(jnp.int32(0) for _ in range(per_tile))),
        )
        firsts = [f - group_block + REACH * per_tile for f in firsts]
        start_row = jnp.full((1, rows), 0, jnp.int32)
        for b in range(per_tile):
            start_row = jnp.where(lane >= b * BLOCK, firsts[b] * BLOCK, start_row)
        last_row = (i + REACH) * rows + lane

        def allowed(j):
            return (key_at >= start_row - j * rows) & (key_at <= last_row - j * rows)

        return firsts[0] // per_tile, allowed

    return masked


def wide_at(j, rows):
    return pl.ds(pl.multiple_of(j * rows, rows), WIDE * rows)


def grad_kernel(
    docs, q_ref, g_ref, k_ref, v_ref, d_ref, l_ref, dq_ref, dk_ref, dv_ref, hk_ref, hv_ref, dk, dv
):
    rows = q_ref.shape[0] // GROUP
    scale = 1.0 / math.sqrt(DH)
    _, shard, _ = place()
    dk[...] = jnp.zeros_like(dk)
    dv[...] = jnp.zeros_like(dv)
    masked = mask_maker(docs, shard - lax.rem(shard, GROUP), rows)

    def tile(i, _):
        begin, allowed = masked(i)
        end = i + REACH + 1
        steps = (end - begin + WIDE - 1) // WIDE
        q = q_ref[rows_at(i, rows), :]
        g = g_ref[rows_at(i, rows), :]
        delta = d_ref[i, 0:1, :]
        logsum = l_ref[i, 0:1, :]

        def grads(c, dq):
            j = end - (c + 1) * WIDE
            at = wide_at(j, rows)
            k = k_ref[at, :]
            s = lax.dot_general(k, q, NT, preferred_element_type=jnp.float32)
            dprob = lax.dot_general(v_ref[at, :], g, NT, preferred_element_type=jnp.float32)
            prob = jnp.exp2(jnp.where(allowed(j), s * EXP2_SCALE - logsum, -1e30))
            ds = (prob * (dprob - delta)).astype(jnp.bfloat16)
            dv[at, :] += jnp.dot(prob.astype(jnp.bfloat16), g, preferred_element_type=jnp.float32)
            dk[at, :] += jnp.dot(ds, q, preferred_element_type=jnp.float32)
            return dq + lax.dot_general(ds, k, TN, preferred_element_type=jnp.float32)

        dq = lax.fori_loop(0, steps, grads, jnp.zeros((rows, DH), jnp.float32))
        dq_ref[rows_at(i, rows), :] = (dq * scale).astype(jnp.bfloat16)
        return 0

    lax.fori_loop(0, GROUP, tile, 0)
    halo = REACH * rows
    hk_ref[...] = (dk[:halo, :] * scale).astype(jnp.bfloat16)
    hv_ref[...] = dv[:halo, :].astype(jnp.bfloat16)
    dk_ref[...] = dk[halo:, :] * scale
    dv_ref[...] = dv[halo:, :]


def collect_kernel(
    dq_ref, dk_ref, dv_ref, hk_ref, hv_ref, qo, ko, vo, hk, hv, ks, vs, send, recv, hsend, hrecv, local
):
    rows = qo.shape[0]
    count, shard, device = place()
    me = lax.rem(shard, GROUP)
    base = shard - me
    ahead = device(lax.rem(shard + GROUP, count))
    behind = device(lax.rem(shard + count - GROUP, count))
    barrier = pltpu.get_barrier_semaphore()
    for j in range(1, GROUP):
        peer = device(base + lax.rem(me + j, GROUP))
        pl.semaphore_signal(barrier, inc=1, device_id=peer, device_id_type=MESH)
    pl.semaphore_signal(barrier, inc=1, device_id=ahead, device_id_type=MESH)
    pl.semaphore_wait(barrier, GROUP)

    halos = ((hk_ref, hk), (hv_ref, hv))

    def halo_copy(which, s):
        src, dst = halos[which]
        at = rows_at(s - 1, rows)
        return pltpu.make_async_remote_copy(
            src_ref=src.at[at, :],
            dst_ref=dst.at[at, :],
            send_sem=hsend.at[which, s],
            recv_sem=hrecv.at[which, s],
            device_id=behind,
            device_id_type=MESH,
        )

    tensors = ((dq_ref, qo), (ks, ko), (vs, vo))

    def out_copy(which, j):
        src, dst = tensors[which]
        peer = lax.rem(me + j, GROUP)
        return pltpu.make_async_remote_copy(
            src_ref=src.at[rows_at(peer, rows), :],
            dst_ref=dst.at[:, cols_at(me)],
            send_sem=send.at[which, j],
            recv_sem=recv.at[which, j],
            device_id=device(base + peer),
            device_id_type=MESH,
        )

    def in_copy(which, j):
        src, dst = tensors[which]
        peer = lax.rem(me + GROUP - j, GROUP)
        return pltpu.make_async_remote_copy(
            src_ref=src.at[rows_at(peer, rows), :],
            dst_ref=dst.at[:, cols_at(peer)],
            send_sem=send.at[which, j],
            recv_sem=recv.at[which, j],
            device_id=device(base + peer),
            device_id_type=MESH,
        )

    def own_copy(which):
        src, dst = tensors[which]
        return pltpu.make_async_copy(
            src.at[rows_at(me, rows), :], dst.at[:, cols_at(me)], local.at[which]
        )

    for j in range(GROUP):
        s = lax.rem(me + j, GROUP)

        @pl.when(s >= 1)
        def _():
            for which in range(2):
                halo_copy(which, s).start()

    own_copy(0).start()
    for j in range(1, GROUP):
        out_copy(0, j).start()

    for j in [*range(1, GROUP), 0]:
        s = lax.rem(me + j, GROUP)
        at = rows_at(s, rows)

        @pl.when(s == 0)
        def _():
            ks[at, :] = dk_ref[at, :].astype(jnp.bfloat16)
            vs[at, :] = dv_ref[at, :].astype(jnp.bfloat16)

        @pl.when(s >= 1)
        def _():
            before = rows_at(s - 1, rows)
            halo_copy(0, s).wait_recv()
            ks[at, :] = (dk_ref[at, :] + hk[before, :].astype(jnp.float32)).astype(jnp.bfloat16)
            halo_copy(1, s).wait_recv()
            vs[at, :] = (dv_ref[at, :] + hv[before, :].astype(jnp.float32)).astype(jnp.bfloat16)

        for which in (1, 2):
            if j:
                out_copy(which, j).start()
            else:
                own_copy(which).start()

    for which in range(3):
        own_copy(which).wait()
        for j in range(1, GROUP):
            in_copy(which, j).wait_recv()
    for which in range(3):
        for j in range(1, GROUP):
            out_copy(which, j).wait_send()
    for s in range(1, GROUP):
        for which in range(2):
            halo_copy(which, s).wait_send()


def per_device(query_rows, key_rows, value_rows, forward_out, out_grad, doc_blocks):
    rows, features = query_rows.shape
    bf16, f32 = jnp.bfloat16, jnp.float32
    own, window = GROUP * rows, (GROUP + REACH) * rows
    vmem = pl.BlockSpec(memory_space=pltpu.VMEM)
    dma = pltpu.SemaphoreType.DMA
    smem = pl.BlockSpec(memory_space=pltpu.SMEM)
    hbm = pl.BlockSpec(memory_space=pltpu.HBM)
    qh, gh, kw, vw, dh, lh = pl.pallas_call(
        spread_kernel,
        out_shape=(
            jax.ShapeDtypeStruct((own, DH), bf16),
            jax.ShapeDtypeStruct((own, DH), bf16),
            jax.ShapeDtypeStruct((window, DH), bf16),
            jax.ShapeDtypeStruct((window, DH), bf16),
            jax.ShapeDtypeStruct((GROUP, 8, rows), f32),
            jax.ShapeDtypeStruct((GROUP, 8, rows), f32),
        ),
        in_specs=[smem] + [hbm] * 5,
        out_specs=[vmem] * 6,
        scratch_shapes=[
            pltpu.VMEM((rows, features), bf16),
            pltpu.VMEM((rows, features), bf16),
            pltpu.VMEM((HEADS, 8, rows), f32),
            dma((5, GROUP)),
            dma((5, GROUP)),
            dma((2, GROUP)),
            dma((2, GROUP)),
            dma((7,)),
        ],
        compiler_params=pltpu.CompilerParams(
            collective_id=0, has_side_effects=True, vmem_limit_bytes=40 << 20
        ),
        name="spread",
    )(doc_blocks, query_rows, key_rows, value_rows, forward_out, out_grad)
    dq, dk, dv, hk, hv = pl.pallas_call(
        grad_kernel,
        out_shape=(
            jax.ShapeDtypeStruct((own, DH), bf16),
            jax.ShapeDtypeStruct((own, DH), f32),
            jax.ShapeDtypeStruct((own, DH), f32),
            jax.ShapeDtypeStruct((window - own, DH), bf16),
            jax.ShapeDtypeStruct((window - own, DH), bf16),
        ),
        in_specs=[smem] + [vmem] * 6,
        out_specs=[vmem] * 5,
        scratch_shapes=[
            pltpu.VMEM((window, DH), f32),
            pltpu.VMEM((window, DH), f32),
        ],
        compiler_params=pltpu.CompilerParams(vmem_limit_bytes=40 << 20),
        name="grad",
    )(doc_blocks, qh, gh, kw, vw, dh, lh)
    return pl.pallas_call(
        collect_kernel,
        out_shape=(jax.ShapeDtypeStruct((rows, features), bf16),) * 3,
        in_specs=[vmem] * 5,
        out_specs=[vmem] * 3,
        scratch_shapes=[
            pltpu.VMEM((window - own, DH), bf16),
            pltpu.VMEM((window - own, DH), bf16),
            pltpu.VMEM((own, DH), bf16),
            pltpu.VMEM((own, DH), bf16),
            dma((3, GROUP)),
            dma((3, GROUP)),
            dma((2, GROUP)),
            dma((2, GROUP)),
            dma((3,)),
        ],
        compiler_params=pltpu.CompilerParams(
            collective_id=1, has_side_effects=True, vmem_limit_bytes=40 << 20
        ),
        name="collect",
    )(dq, dk, dv, hk, hv)


def solution(mesh):
    rows = P(("cx", "cy"), None)
    return jax.shard_map(
        per_device,
        mesh=mesh,
        in_specs=(rows, rows, rows, rows, rows, P()),
        out_specs=(rows, rows, rows),
        check_vma=False,
    )
```

```python
import math

import jax
import jax.numpy as jnp
from jax import lax
from jax.experimental import pallas as pl
from jax.experimental.pallas import tpu as pltpu
from jax.sharding import PartitionSpec as P

HEADS = 8
DH = 128
BLOCK = 128
REACH = 7
GROUP = 8
WIDE = 2
EXP2_SCALE = math.log2(math.e) / math.sqrt(DH)
MESH = pl.DeviceIdType.MESH
NT = (((1,), (1,)), ((), ()))
TN = (((0,), (0,)), ((), ()))


def place():
    inner = lax.axis_size("cy")
    count = lax.axis_size("cx") * inner
    shard = lax.axis_index("cx") * inner + lax.axis_index("cy")

    def device(index):
        return (index // inner, lax.rem(index, inner))

    return count, shard, device


def rows_at(index, rows):
    return pl.ds(pl.multiple_of(index * rows, rows), rows)


def cols_at(head):
    return pl.ds(pl.multiple_of(head * DH, DH), DH)


def spread_kernel(
    docs, q_ref, k_ref, v_ref, o_ref, g_ref, qh, gh, kw, vw, dh, lh,
    o_here, g_here, dsend, send, recv, fsend, frecv, local
):
    rows = q_ref.shape[0]
    count, shard, device = place()
    me = lax.rem(shard, GROUP)
    base = shard - me
    ahead = device(lax.rem(shard + GROUP, count))
    behind = device(lax.rem(shard + count - GROUP, count))
    tensors = ((k_ref, kw, REACH), (v_ref, vw, REACH), (q_ref, qh, 0), (g_ref, gh, 0))
    K, V, Q, G, DELTA = range(5)

    def out_copy(which, j):
        src, dst, shift = tensors[which]
        peer = lax.rem(me + j, GROUP)
        return pltpu.make_async_remote_copy(
            src_ref=src.at[:, cols_at(peer)],
            dst_ref=dst.at[rows_at(me + shift, rows), :],
            send_sem=send.at[which, j],
            recv_sem=recv.at[which, j],
            device_id=device(base + peer),
            device_id_type=MESH,
        )

    def in_copy(which, j):
        src, dst, shift = tensors[which]
        peer = lax.rem(me + GROUP - j, GROUP)
        return pltpu.make_async_remote_copy(
            src_ref=src.at[:, cols_at(peer)],
            dst_ref=dst.at[rows_at(peer + shift, rows), :],
            send_sem=send.at[which, j],
            recv_sem=recv.at[which, j],
            device_id=device(base + peer),
            device_id_type=MESH,
        )

    def own_copy(which):
        src, dst, shift = tensors[which]
        return pltpu.make_async_copy(
            src.at[:, cols_at(me)], dst.at[rows_at(me + shift, rows), :], local.at[which]
        )

    def forward(which, shard_in_group):
        _, dst, shift = tensors[which]
        return pltpu.make_async_remote_copy(
            src_ref=dst.at[rows_at(shard_in_group + shift, rows), :],
            dst_ref=dst.at[rows_at(shard_in_group - 1, rows), :],
            send_sem=fsend.at[which, shard_in_group],
            recv_sem=frecv.at[which, shard_in_group],
            device_id=ahead,
            device_id_type=MESH,
        )

    def forward_own(which):
        own_copy(which).wait()

        @pl.when(me >= 1)
        def _():
            forward(which, me).start()

    def forward_from(which, j):
        source = lax.rem(me + GROUP - j, GROUP)
        in_copy(which, j).wait_recv()

        @pl.when(source >= 1)
        def _():
            forward(which, source).start()

    def forward_all(which):
        forward_own(which)
        for j in range(1, GROUP):
            forward_from(which, j)

    g_copy = pltpu.make_async_copy(g_ref, g_here, local.at[5])
    o_copy = pltpu.make_async_copy(o_ref, o_here, local.at[6])
    barrier = pltpu.get_barrier_semaphore()
    for j in range(1, GROUP):
        peer = device(base + lax.rem(me + j, GROUP))
        pl.semaphore_signal(barrier, inc=1, device_id=peer, device_id_type=MESH)
    pl.semaphore_signal(barrier, inc=1, device_id=behind, device_id_type=MESH)
    for which in range(4):
        own_copy(which).start()
    g_copy.start()
    o_copy.start()
    pl.semaphore_wait(barrier, GROUP)

    for which in (K, Q):
        for j in range(1, GROUP):
            out_copy(which, j).start()

    g_copy.wait()
    o_copy.wait()
    ones = jnp.ones((8, DH), jnp.bfloat16)
    for head in range(HEADS):
        cols = slice(head * DH, (head + 1) * DH)
        product = g_here[:, cols].astype(jnp.float32) * o_here[:, cols].astype(jnp.float32)
        high = product.astype(jnp.bfloat16)
        low = (product - high.astype(jnp.float32)).astype(jnp.bfloat16)
        dsend[head] = lax.dot_general(
            ones, high, NT, preferred_element_type=jnp.float32
        ) + lax.dot_general(ones, low, NT, preferred_element_type=jnp.float32)

    def delta_copy(j, peer, source):
        return pltpu.make_async_remote_copy(
            src_ref=dsend.at[peer],
            dst_ref=dh.at[source],
            send_sem=send.at[DELTA, j],
            recv_sem=recv.at[DELTA, j],
            device_id=device(base + peer),
            device_id_type=MESH,
        )

    own_delta = pltpu.make_async_copy(dsend.at[me], dh.at[me], local.at[DELTA])
    own_delta.start()
    for j in range(1, GROUP):
        delta_copy(j, lax.rem(me + j, GROUP), me).start()

    forward_all(K)
    for which in (V, G):
        for j in range(1, GROUP):
            out_copy(which, j).start()
    forward_own(V)
    own_copy(Q).wait()
    for j in range(1, GROUP):
        in_copy(Q, j).wait_recv()
    for s in range(1, GROUP):
        forward(K, s).wait_recv()

    masked = mask_maker(docs, base, rows)

    def stats(i, _):
        _, allowed = masked(i)
        q = qh[rows_at(i, rows), :]
        top = jnp.full((1, rows), -1e30, jnp.float32)
        total = jnp.zeros((1, rows), jnp.float32)
        for c in range((REACH + 1) // WIDE):
            j = i + c * WIDE
            s = lax.dot_general(
                kw[wide_at(j, rows), :], q, NT, preferred_element_type=jnp.float32
            )
            s = jnp.where(allowed(j), s * EXP2_SCALE, -1e30)
            higher = jnp.maximum(top, jnp.max(s, axis=0, keepdims=True))
            total = total * jnp.exp2(top - higher) + jnp.sum(
                jnp.exp2(s - higher), axis=0, keepdims=True
            )
            top = higher
        lh[i] = jnp.broadcast_to(top + jnp.log2(total), (8, rows))

        @pl.when(i >= 1)
        def _():
            forward_from(V, i)

        return 0

    lax.fori_loop(0, GROUP, stats, 0)
    own_copy(G).wait()
    for j in range(1, GROUP):
        in_copy(G, j).wait_recv()
    own_delta.wait()
    for j in range(1, GROUP):
        peer = lax.rem(me + GROUP - j, GROUP)
        delta_copy(j, peer, peer).wait_recv()
    for s in range(1, GROUP):
        forward(V, s).wait_recv()
    for s in range(1, GROUP):
        for which in (K, V):
            forward(which, s).wait_send()
    for j in range(1, GROUP):
        for which in range(4):
            out_copy(which, j).wait_send()
        delta_copy(j, lax.rem(me + j, GROUP), me).wait_send()


def mask_maker(docs, base, rows):
    per_tile = rows // BLOCK
    group_block = base * per_tile
    key_at = lax.broadcasted_iota(jnp.int32, (WIDE * rows, rows), 0)
    lane = lax.broadcasted_iota(jnp.int32, (1, rows), 1)

    def masked(i):
        first_block = group_block + i * per_tile

        def look(n, state):
            start, firsts = state
            firsts = tuple(
                jnp.where(start <= first_block + b, start, firsts[b]) for b in range(per_tile)
            )
            return start + docs[n], firsts

        _, firsts = lax.fori_loop(
            0,
            docs.shape[0],
            look,
            (jnp.int32(0), tuple(jnp.int32(0) for _ in range(per_tile))),
        )
        firsts = [f - group_block + REACH * per_tile for f in firsts]
        start_row = jnp.full((1, rows), 0, jnp.int32)
        for b in range(per_tile):
            start_row = jnp.where(lane >= b * BLOCK, firsts[b] * BLOCK, start_row)
        last_row = (i + REACH) * rows + lane

        def allowed(j):
            return (key_at >= start_row - j * rows) & (key_at <= last_row - j * rows)

        return firsts[0] // per_tile, allowed

    return masked


def wide_at(j, rows):
    return pl.ds(pl.multiple_of(j * rows, rows), WIDE * rows)


def grad_kernel(
    docs, q_ref, g_ref, k_ref, v_ref, d_ref, l_ref, dq_ref, dk_ref, dv_ref, hk_ref, hv_ref, dk, dv
):
    rows = q_ref.shape[0] // GROUP
    scale = 1.0 / math.sqrt(DH)
    _, shard, _ = place()
    dk[...] = jnp.zeros_like(dk)
    dv[...] = jnp.zeros_like(dv)
    masked = mask_maker(docs, shard - lax.rem(shard, GROUP), rows)

    def tile(i, _):
        begin, allowed = masked(i)
        end = i + REACH + 1
        steps = (end - begin + WIDE - 1) // WIDE
        q = q_ref[rows_at(i, rows), :]
        g = g_ref[rows_at(i, rows), :]
        delta = d_ref[i, 0:1, :]
        logsum = l_ref[i, 0:1, :]

        def grads(c, dq):
            j = end - (c + 1) * WIDE
            at = wide_at(j, rows)
            k = k_ref[at, :]
            s = lax.dot_general(k, q, NT, preferred_element_type=jnp.float32)
            dprob = lax.dot_general(v_ref[at, :], g, NT, preferred_element_type=jnp.float32)
            prob = jnp.exp2(jnp.where(allowed(j), s * EXP2_SCALE - logsum, -1e30))
            ds = (prob * (dprob - delta)).astype(jnp.bfloat16)
            dv[at, :] += jnp.dot(prob.astype(jnp.bfloat16), g, preferred_element_type=jnp.float32)
            dk[at, :] += jnp.dot(ds, q, preferred_element_type=jnp.float32)
            return dq + lax.dot_general(ds, k, TN, preferred_element_type=jnp.float32)

        dq = lax.fori_loop(0, steps, grads, jnp.zeros((rows, DH), jnp.float32))
        dq_ref[rows_at(i, rows), :] = (dq * scale).astype(jnp.bfloat16)
        return 0

    lax.fori_loop(0, GROUP, tile, 0)
    halo = REACH * rows
    hk_ref[...] = (dk[:halo, :] * scale).astype(jnp.bfloat16)
    hv_ref[...] = dv[:halo, :].astype(jnp.bfloat16)
    dk_ref[...] = dk[halo:, :] * scale
    dv_ref[...] = dv[halo:, :]


def collect_kernel(
    dq_ref, dk_ref, dv_ref, hk_ref, hv_ref, qo, ko, vo, hk, hv, ks, vs, send, recv, hsend, hrecv, local
):
    rows = qo.shape[0]
    count, shard, device = place()
    me = lax.rem(shard, GROUP)
    base = shard - me
    ahead = device(lax.rem(shard + GROUP, count))
    behind = device(lax.rem(shard + count - GROUP, count))
    barrier = pltpu.get_barrier_semaphore()
    for j in range(1, GROUP):
        peer = device(base + lax.rem(me + j, GROUP))
        pl.semaphore_signal(barrier, inc=1, device_id=peer, device_id_type=MESH)
    pl.semaphore_signal(barrier, inc=1, device_id=ahead, device_id_type=MESH)
    pl.semaphore_wait(barrier, GROUP)

    halos = ((hk_ref, hk), (hv_ref, hv))

    def halo_copy(which, s):
        src, dst = halos[which]
        at = rows_at(s - 1, rows)
        return pltpu.make_async_remote_copy(
            src_ref=src.at[at, :],
            dst_ref=dst.at[at, :],
            send_sem=hsend.at[which, s],
            recv_sem=hrecv.at[which, s],
            device_id=behind,
            device_id_type=MESH,
        )

    tensors = ((dq_ref, qo), (ks, ko), (vs, vo))

    def out_copy(which, j):
        src, dst = tensors[which]
        peer = lax.rem(me + j, GROUP)
        return pltpu.make_async_remote_copy(
            src_ref=src.at[rows_at(peer, rows), :],
            dst_ref=dst.at[:, cols_at(me)],
            send_sem=send.at[which, j],
            recv_sem=recv.at[which, j],
            device_id=device(base + peer),
            device_id_type=MESH,
        )

    def in_copy(which, j):
        src, dst = tensors[which]
        peer = lax.rem(me + GROUP - j, GROUP)
        return pltpu.make_async_remote_copy(
            src_ref=src.at[rows_at(peer, rows), :],
            dst_ref=dst.at[:, cols_at(peer)],
            send_sem=send.at[which, j],
            recv_sem=recv.at[which, j],
            device_id=device(base + peer),
            device_id_type=MESH,
        )

    def own_copy(which):
        src, dst = tensors[which]
        return pltpu.make_async_copy(
            src.at[rows_at(me, rows), :], dst.at[:, cols_at(me)], local.at[which]
        )

    for j in range(GROUP):
        s = lax.rem(me + j, GROUP)

        @pl.when(s >= 1)
        def _():
            for which in range(2):
                halo_copy(which, s).start()

    own_copy(0).start()
    for j in range(1, GROUP):
        out_copy(0, j).start()

    for j in [*range(1, GROUP), 0]:
        s = lax.rem(me + j, GROUP)
        at = rows_at(s, rows)

        @pl.when(s == 0)
        def _():
            ks[at, :] = dk_ref[at, :].astype(jnp.bfloat16)
            vs[at, :] = dv_ref[at, :].astype(jnp.bfloat16)

        @pl.when(s >= 1)
        def _():
            before = rows_at(s - 1, rows)
            halo_copy(0, s).wait_recv()
            ks[at, :] = (dk_ref[at, :] + hk[before, :].astype(jnp.float32)).astype(jnp.bfloat16)
            halo_copy(1, s).wait_recv()
            vs[at, :] = (dv_ref[at, :] + hv[before, :].astype(jnp.float32)).astype(jnp.bfloat16)

        for which in (1, 2):
            if j:
                out_copy(which, j).start()
            else:
                own_copy(which).start()

    for which in range(3):
        own_copy(which).wait()
        for j in range(1, GROUP):
            in_copy(which, j).wait_recv()
    for which in range(3):
        for j in range(1, GROUP):
            out_copy(which, j).wait_send()
    for s in range(1, GROUP):
        for which in range(2):
            halo_copy(which, s).wait_send()


def per_device(query_rows, key_rows, value_rows, forward_out, out_grad, doc_blocks):
    rows, features = query_rows.shape
    bf16, f32 = jnp.bfloat16, jnp.float32
    own, window = GROUP * rows, (GROUP + REACH) * rows
    vmem = pl.BlockSpec(memory_space=pltpu.VMEM)
    dma = pltpu.SemaphoreType.DMA
    smem = pl.BlockSpec(memory_space=pltpu.SMEM)
    hbm = pl.BlockSpec(memory_space=pltpu.HBM)
    qh, gh, kw, vw, dh, lh = pl.pallas_call(
        spread_kernel,
        out_shape=(
            jax.ShapeDtypeStruct((own, DH), bf16),
            jax.ShapeDtypeStruct((own, DH), bf16),
            jax.ShapeDtypeStruct((window, DH), bf16),
            jax.ShapeDtypeStruct((window, DH), bf16),
            jax.ShapeDtypeStruct((GROUP, 8, rows), f32),
            jax.ShapeDtypeStruct((GROUP, 8, rows), f32),
        ),
        in_specs=[smem] + [hbm] * 5,
        out_specs=[vmem] * 6,
        scratch_shapes=[
            pltpu.VMEM((rows, features), bf16),
            pltpu.VMEM((rows, features), bf16),
            pltpu.VMEM((HEADS, 8, rows), f32),
            dma((5, GROUP)),
            dma((5, GROUP)),
            dma((2, GROUP)),
            dma((2, GROUP)),
            dma((7,)),
        ],
        compiler_params=pltpu.CompilerParams(
            collective_id=0, has_side_effects=True, vmem_limit_bytes=60 << 20
        ),
        name="spread",
    )(doc_blocks, query_rows, key_rows, value_rows, forward_out, out_grad)
    dq, dk, dv, hk, hv = pl.pallas_call(
        grad_kernel,
        out_shape=(
            jax.ShapeDtypeStruct((own, DH), bf16),
            jax.ShapeDtypeStruct((own, DH), f32),
            jax.ShapeDtypeStruct((own, DH), f32),
            jax.ShapeDtypeStruct((window - own, DH), bf16),
            jax.ShapeDtypeStruct((window - own, DH), bf16),
        ),
        in_specs=[smem] + [vmem] * 6,
        out_specs=[vmem] * 5,
        scratch_shapes=[
            pltpu.VMEM((window, DH), f32),
            pltpu.VMEM((window, DH), f32),
        ],
        compiler_params=pltpu.CompilerParams(vmem_limit_bytes=60 << 20),
        name="grad",
    )(doc_blocks, qh, gh, kw, vw, dh, lh)
    return pl.pallas_call(
        collect_kernel,
        out_shape=(jax.ShapeDtypeStruct((rows, features), bf16),) * 3,
        in_specs=[vmem] * 5,
        out_specs=[vmem] * 3,
        scratch_shapes=[
            pltpu.VMEM((window - own, DH), bf16),
            pltpu.VMEM((window - own, DH), bf16),
            pltpu.VMEM((own, DH), bf16),
            pltpu.VMEM((own, DH), bf16),
            dma((3, GROUP)),
            dma((3, GROUP)),
            dma((2, GROUP)),
            dma((2, GROUP)),
            dma((3,)),
        ],
        compiler_params=pltpu.CompilerParams(
            collective_id=1, has_side_effects=True, vmem_limit_bytes=60 << 20
        ),
        name="collect",
    )(dq, dk, dv, hk, hv)


def solution(mesh):
    rows = P(("cx", "cy"), None)
    return jax.shard_map(
        per_device,
        mesh=mesh,
        in_specs=(rows, rows, rows, rows, rows, P()),
        out_specs=(rows, rows, rows),
        check_vma=False,
    )
```
